32 devices in a mesh: groups: 2 (over y), row: 8 (over z, core), col: 2 (over x).
Axes of the slice: x: 2, y: 2, z: 4, core: 2. Of those that a mesh axis runs over, the one named last changes fastest.
Arguments:
- pair: bfloat16 [160, 80, 128], P(('groups', 'row'), 'col'), parts along dimension 0, may hold values from -6 to 6
- chain: int32 [160], P('groups'), parts along dimension 0, may hold values from -1 to 3
- in_gain: float32 [2, 128], replicated, may hold values from 0.1 to 1.9
- in_proj: bfloat16 [2, 128, 640], replicated, may hold values from -3 to 3
- out_gain: float32 [2, 128], replicated, may hold values from 0.1 to 1.9
- out_proj: bfloat16 [2, 128, 128], replicated, may hold values from -3 to 3
Outputs:
- pair_out: bfloat16 [160, 80, 128], P(('groups', 'row'), 'col'), parts along dimension 0
The draws below stay inside these ranges and needn't reach their ends.
There are 2 independent parts, one for each index of `groups`. The reference program is written for one: setup_inputs(seed, part) draws one part's arguments, and reference() takes and returns one part's arrays. A program takes and returns all parts, laid end to end along the dimension named above; an argument that names none is the same for every part. Nothing has to cross between parts.
Inputs may be any that keep to these rules, and one draw needn't show every extreme that they name: Residue i is padding when chain[i] is negative.
All inputs are finite; a program needn't handle non-finite values.
Results may differ from the reference program's by a relative error of at most 0.0085.
Values may be sent and summed in bfloat16 or wider, within the bound.
A program may use at most 64 MiB of HBM per device.

```python
import jax
import jax.numpy as jnp
from jax import lax

C = 128
CH = 128
RI = 10
N = 80
N_ROW = 8


def chosen_channels(key):
    key = jax.random.fold_in(key, 41)
    first, second = jax.random.split(key, 2)
    order_one = jax.random.permutation(first, CH)
    order_two = jax.random.permutation(second, CH)
    picked = jnp.stack([order_one < CH // 8, order_two < CH // 8], axis=0)
    return picked.astype(jnp.float32)


def base_values(key, shape, spread):
    values = jax.random.truncated_normal(key, -4.0, 4.0, shape, jnp.float32)
    return values * spread


def draw_in_proj(key, part):
    picked = chosen_channels(key)
    key = jax.random.fold_in(key, 3)
    first, second = jax.random.split(key, 2)
    values = base_values(first, (2, C, 4 * CH + C), C ** (-0.5))
    boost = jax.random.uniform(second, (2, CH), jnp.float32, 1.4, 2.0)
    factor = 1.0 + picked * (boost - 1.0)
    drawn = jnp.ones((2, CH), jnp.float32)
    column = jnp.concatenate([drawn, factor, drawn, factor, jnp.ones((2, C), jnp.float32)], axis=1)
    return (values * column[:, None, :]).astype(jnp.bfloat16)


def draw_out_proj(key, part):
    picked = chosen_channels(key)
    key = jax.random.fold_in(key, 5)
    first, second = jax.random.split(key, 2)
    values = base_values(first, (2, CH, C), CH ** (-0.5))
    shrink = jax.random.uniform(second, (2, CH), jnp.float32, 0.015, 0.025)
    factor = 1.0 + picked * (shrink - 1.0)
    return (values * factor[:, :, None]).astype(jnp.bfloat16)


def place_ends(result, own_key, least, largest):
    extent = result.shape
    index_at = [jax.random.randint(jax.random.fold_in(own_key, axis), (), 0, extent[axis]) for axis in range(len(extent))]
    result = result.at[tuple(index_at)].set(least)
    longest = extent.index(max(extent))
    index_at[longest] = (index_at[longest] + 1) % extent[longest]
    return result.at[tuple(index_at)].set(largest)


def block_levels(key, shape, cuts, least, largest):
    def one(axis_at, parts):
        draws = jax.random.uniform(jax.random.fold_in(jax.random.fold_in(key, 6), axis_at), (parts,), jnp.float32, least / len(cuts), largest / len(cuts))
        return jnp.repeat(jnp.exp(draws), shape[axis_at] // parts).reshape((-1,) + (1,) * (len(shape) - axis_at - 1))

    factor_of = one(*cuts[0])
    for cut in cuts[1:]:
        factor_of = factor_of * one(*cut)
    return factor_of


def centred(key, dims, deviation, bound, cuts=(), kind=jnp.bfloat16):
    level = block_levels(key, dims, cuts, -0.22, 0.18) if cuts else 1.0
    entries = jax.random.normal(key, dims, jnp.float32) * deviation * level
    return jnp.minimum(jnp.maximum(entries, -bound), bound).astype(kind)


def setup_inputs(seed: int = 0, part: int = 0) -> dict:
    splits = jax.random.split(jax.random.key(seed), 7)
    part_keys = jax.random.split(jax.random.fold_in(splits[6], part), 7)
    return {
        "pair": centred(part_keys[0], (N, N, C), 1.0, 6.0, ((0, 8), (1, 2))),
        "chain": place_ends(jax.random.randint(part_keys[1], (N,), -1, 4), jax.random.fold_in(part_keys[1], 1), -1, 3).astype(jnp.int32),
        "in_gain": jnp.clip(1.0 + 0.18 * jax.random.normal(splits[2], (2, C), jnp.float32), 0.1, 1.9),
        "in_proj": draw_in_proj(jax.random.fold_in(splits[6], 71), part),
        "out_gain": jnp.clip(1.0 + 0.18 * jax.random.normal(splits[4], (2, CH), jnp.float32), 0.1, 1.9),
        "out_proj": draw_out_proj(jax.random.fold_in(splits[6], 71), part),
    }


def normalize(values, gain):
    mean = lax.optimization_barrier(jnp.mean(values, axis=-1, keepdims=True))
    centered = values - mean
    spread = lax.optimization_barrier(jnp.mean(centered * centered, axis=-1, keepdims=True))
    return centered * lax.rsqrt(spread + 1e-05) * gain

def branch_terms(block, rows_valid, cols_valid, gain, weights):
    normed = normalize(block.astype(jnp.float32), gain).astype(jnp.bfloat16)
    flat = normed.reshape(-1, normed.shape[-1])
    proj = jnp.dot(flat, weights, preferred_element_type=jnp.float32)
    proj = proj.reshape(block.shape[0], block.shape[1], -1)
    mask = (rows_valid[:, None] * cols_valid[None, :])[:, :, None]
    left = (jax.nn.sigmoid(proj[..., 0:CH]) * proj[..., CH:2 * CH] * mask).astype(jnp.bfloat16)
    right = (jax.nn.sigmoid(proj[..., 2 * CH:3 * CH]) * proj[..., 3 * CH:4 * CH] * mask).astype(jnp.bfloat16)
    gate = jax.nn.sigmoid(proj[..., 4 * CH:4 * CH + C])
    return (left, right, gate)

def one_update(pair, valid, gain, weights, tri_gain, out_weights, incoming):
    blocks = pair.reshape(N_ROW, RI, N, C)
    valid_rows = valid.reshape(N_ROW, RI)

    def per_block(items):
        return branch_terms(items[0], items[1], valid, gain, weights)
    left, right, gate = lax.map(per_block, (blocks, valid_rows))
    left = left.reshape(N, N, CH)
    right = right.reshape(N, N, CH)
    gate = gate.reshape(N, N, C)
    if incoming:
        tri = jnp.einsum('kic,kjc->ijc', left.astype(jnp.float32), right.astype(jnp.float32))
    else:
        tri = jnp.einsum('ikc,jkc->ijc', left.astype(jnp.float32), right.astype(jnp.float32))
    tri_normed = normalize(tri, tri_gain).astype(jnp.bfloat16)
    projected = jnp.dot(tri_normed.reshape(-1, CH), out_weights, preferred_element_type=jnp.float32)
    update = gate * projected.reshape(N, N, C)
    return (pair.astype(jnp.float32) + update).astype(jnp.bfloat16)

def reference(pair, chain, in_gain, in_proj, out_gain, out_proj):
    valid = (chain >= 0).astype(jnp.float32)
    pair_mid = one_update(pair, valid, in_gain[0], in_proj[0], out_gain[0], out_proj[0], False)
    return one_update(pair_mid, valid, in_gain[1], in_proj[1], out_gain[1], out_proj[1], True)
```

```python
import functools

import jax
import jax.numpy as jnp
from jax import lax
from jax.experimental import pallas as pl
from jax.experimental.pallas import tpu as pltpu
from jax.sharding import PartitionSpec as P

C = 128
CH = 128
F32 = jnp.float32
BF16 = jnp.bfloat16
MESH = pl.DeviceIdType.MESH


def normalize(values, gain):
    mean = jnp.mean(values, axis=-1, keepdims=True)
    centered = values - mean
    spread = jnp.mean(centered * centered, axis=-1, keepdims=True)
    return centered * lax.rsqrt(spread + 1e-05) * gain


def branch_terms(tile, rows_valid, cols_valid, gain, weights):
    normed = normalize(tile.astype(jnp.float32), gain).astype(jnp.bfloat16)
    flat = normed.reshape(-1, normed.shape[-1])
    proj = jnp.dot(flat, weights, preferred_element_type=jnp.float32)
    proj = proj.reshape(tile.shape[0], tile.shape[1], -1)
    mask = (rows_valid[:, None] * cols_valid[None, :])[:, :, None]
    left = (jax.nn.sigmoid(proj[..., 0:CH]) * proj[..., CH : 2 * CH] * mask).astype(jnp.bfloat16)
    right = (jax.nn.sigmoid(proj[..., 2 * CH : 3 * CH]) * proj[..., 3 * CH : 4 * CH] * mask).astype(
        jnp.bfloat16
    )
    gate = jax.nn.sigmoid(proj[..., 4 * CH : 4 * CH + C])
    return (left, right, gate)


def finish(tile, tri, gate, tri_gain, out_weights):
    tri_normed = normalize(tri, tri_gain).astype(jnp.bfloat16)
    projected = jnp.dot(
        tri_normed.reshape(-1, tri.shape[-1]), out_weights, preferred_element_type=jnp.float32
    )
    update = gate * projected.reshape(gate.shape)
    return (tile.astype(jnp.float32) + update).astype(jnp.bfloat16)


def outgoing(tile, rows_valid, cols_valid, gain, weights, tri_gain, out_weights):
    left, right, gate = branch_terms(tile, rows_valid, cols_valid, gain, weights)
    right_cols = lax.all_gather(right, "row", axis=0, tiled=True)
    right_rows = lax.all_to_all(right_cols, "col", split_axis=0, concat_axis=1, tiled=True)
    tri = jnp.einsum(
        "ikc,jkc->ijc",
        lax.all_gather(left, "col", axis=1, tiled=True),
        right_rows,
        preferred_element_type=jnp.float32,
    )
    return finish(tile, tri, gate, tri_gain, out_weights)


def incoming(tile, rows_valid, cols_valid, gain, weights, tri_gain, out_weights):
    left, right, gate = branch_terms(tile, rows_valid, cols_valid, gain, weights)
    strip = lax.all_gather(left, "col", axis=1, tiled=True)
    left_cols = lax.all_to_all(strip, "row", split_axis=1, concat_axis=0, tiled=True)
    tri = jnp.einsum(
        "kic,kjc->ijc",
        left_cols,
        lax.all_gather(right, "row", axis=0, tiled=True),
        preferred_element_type=jnp.float32,
    )
    return finish(tile, tri, gate, tri_gain, out_weights)


def body(pair, chain, in_gain, in_proj, out_gain, out_proj):
    row_count = pair.shape[0]
    col_count = pair.shape[1]
    valid = (chain >= 0).astype(jnp.float32)
    rows_valid = lax.dynamic_slice_in_dim(valid, lax.axis_index("row") * row_count, row_count, 0)
    cols_valid = lax.dynamic_slice_in_dim(valid, lax.axis_index("col") * col_count, col_count, 0)
    pair_mid = outgoing(
        pair, rows_valid, cols_valid, in_gain[0], in_proj[0], out_gain[0], out_proj[0]
    )
    return incoming(
        pair_mid, rows_valid, cols_valid, in_gain[1], in_proj[1], out_gain[1], out_proj[1]
    )


def layer_norm(values, gain):
    mean = jnp.mean(values, axis=-1, keepdims=True)
    centered = values - mean
    spread = jnp.mean(centered * centered, axis=-1, keepdims=True)
    return (centered * lax.rsqrt(spread + 1e-05) * gain).astype(BF16)


def kernel(
    n_row,
    ri,
    ci,
    cuts,
    pair_ref,
    chain_ref,
    in_gain,
    in_proj,
    out_gain,
    out_proj,
    out_ref,
    slots0,
    slots1,
    piece_out,
    piece_in,
    piece_f32,
    left_f32,
    acc,
    tri,
    half_out,
    half_in,
    gate_ref,
    mask_ref,
    send_sem,
    recv_sem,
    piece_send,
    piece_recv,
    half_send,
    half_recv,
):
    g = lax.axis_index("groups")
    r = lax.axis_index("row")
    c = lax.axis_index("col")
    n_z = n_row // 2
    per = ci // ri
    z = r // 2
    k = r % 2
    cells = ri * ci

    barrier = pltpu.get_barrier_semaphore()
    for dr in range(n_row):
        for dc in range(2):
            if dr or dc:
                pl.semaphore_signal(
                    barrier,
                    inc=1,
                    device_id=(g, lax.rem(r + dr, n_row), lax.rem(c + dc, 2)),
                    device_id_type=MESH,
                )

    shape = (ri, ci, n_row * ri)
    lane = lax.broadcasted_iota(jnp.int32, shape, 2)
    row_at = lax.broadcasted_iota(jnp.int32, shape, 0) + r * ri
    col_at = lax.broadcasted_iota(jnp.int32, shape, 1) + c * ci
    padding = jnp.where(chain_ref[...] < 0, 1.0, 0.0).astype(F32).reshape(1, 1, -1)
    hit = jnp.where((lane == row_at) | (lane == col_at), padding, 0.0)
    mask_ref[...] = 1.0 - jnp.max(hit.reshape(cells, -1), axis=-1, keepdims=True)

    def project(normed, u, first, count):
        return jnp.dot(
            normed,
            in_proj[u, :, first * CH : (first + count) * CH],
            preferred_element_type=F32,
        )

    def gated(both):
        return jax.nn.sigmoid(both[:, :CH]) * both[:, CH:] * mask_ref[...]

    def gather_copy(u, slots, row, cut, way, target):
        lo, hi = cuts[cut], cuts[cut + 1]
        part = slots.at[row, pl.ds(lo, hi - lo)]
        return pltpu.make_async_remote_copy(
            src_ref=part,
            dst_ref=part,
            send_sem=send_sem.at[u, way, row, cut],
            recv_sem=recv_sem.at[u, row, cut],
            device_id=target,
            device_id_type=MESH,
        )

    n_cut = len(cuts) - 1
    up = (g, lax.rem(r + 2, n_row), c)
    down = (g, lax.rem(r + n_row - 2, n_row), c)
    other = (g, r + 1 - 2 * k, c)

    def forward(u, slots, row, cut, goes_up, goes_down, act):
        @pl.when(goes_up)
        def _():
            act(gather_copy(u, slots, row, cut, 0, up))

        @pl.when(goes_down)
        def _():
            act(gather_copy(u, slots, row, cut, 1, down))

        act(gather_copy(u, slots, row, cut, 2, other))

    def each_arrival(visit):
        for dist in range(1, n_z):

            @pl.when(z >= dist)
            def _():
                visit(z - dist, 0)

            @pl.when(z + dist < n_z)
            def _():
                visit(z + dist, 1)

    def start(copy):
        copy.start()

    def end(copy):
        copy.wait_send()

    def send_own(u, slots):
        for cut in range(n_cut):
            forward(u, slots, r, cut, z < n_z - 1, z > 0, start)

    def gather(u, slots, work):
        work(r)
        for cut in range(n_cut):
            gather_copy(u, slots, r + 1 - 2 * k, cut, 2, other).wait_recv()
        work(r + 1 - 2 * k)

        def visit(z_from, side):
            mine = 2 * z_from + k
            theirs = 2 * z_from + 1 - k
            for cut in range(n_cut):
                gather_copy(u, slots, mine, cut, 2, other).wait_recv()
                if side == 0:
                    forward(u, slots, mine, cut, z < n_z - 1, False, start)
                else:
                    forward(u, slots, mine, cut, False, z > 0, start)
            work(mine)
            for cut in range(n_cut):
                gather_copy(u, slots, theirs, cut, 2, other).wait_recv()
            work(theirs)

        each_arrival(visit)

    def finish_sends(u, slots):
        for cut in range(n_cut):
            forward(u, slots, r, cut, z < n_z - 1, z > 0, end)

        def visit(z_from, side):
            for cut in range(n_cut):
                if side == 0:
                    forward(u, slots, 2 * z_from + k, cut, z < n_z - 1, False, end)
                else:
                    forward(u, slots, 2 * z_from + k, cut, False, z > 0, end)

        each_arrival(visit)

    def finish_update(u, tile):
        normed = layer_norm(tri[...].reshape(cells, CH), out_gain[u : u + 1, :])
        projected = jnp.dot(normed, out_proj[u], preferred_element_type=F32)
        return (tile.astype(F32) + gate_ref[...] * projected).astype(BF16)

    normed = layer_norm(pair_ref[...].astype(F32), in_gain[0:1, :])
    slots0[r] = gated(project(normed, 0, 2, 2)).astype(BF16)
    pl.semaphore_wait(barrier, 2 * n_row - 1)
    send_own(0, slots0)
    left_f32[...] = gated(project(normed, 0, 0, 2)).astype(BF16).astype(F32).reshape(ri, ci, CH)
    gate_ref[...] = jax.nn.sigmoid(project(normed, 0, 4, 1))

    def outgoing_block(row):
        block = slots0[row].astype(F32).reshape(ri, ci, CH)
        for i in range(ri):
            acc[row, i] = jnp.sum(left_f32[i][None] * block, axis=1)

    gather(0, slots0, outgoing_block)

    def assemble(half):
        for q in range(per):
            tri[:, q * ri : (q + 1) * ri, :] = acc[half * per + q]

    assemble(1 - c)
    half_out[...] = tri[...].reshape(cells, CH).astype(BF16)
    half_copy = pltpu.make_async_remote_copy(
        src_ref=half_out,
        dst_ref=half_in,
        send_sem=half_send,
        recv_sem=half_recv,
        device_id=(g, r, 1 - c),
        device_id_type=MESH,
    )
    half_copy.start()
    assemble(c)
    half_copy.wait_recv()
    tri[...] = tri[...] + half_in[...].astype(F32).reshape(ri, ci, CH)
    mid = finish_update(0, pair_ref[...])
    out_ref[...] = mid

    normed = layer_norm(mid.astype(F32), in_gain[1:2, :])
    slots1[r] = gated(project(normed, 1, 2, 2)).astype(BF16)
    send_own(1, slots1)
    left_f32[...] = gated(project(normed, 1, 0, 2)).reshape(ri, ci, CH)
    used = ri * ri
    for q in range(per):
        for kk in range(ri):
            piece_f32[q, kk * ri : (kk + 1) * ri, :] = left_f32[kk, q * ri : (q + 1) * ri, :]
        piece_out[q, :, :] = piece_f32[q].astype(BF16)

    def piece_copy(q, col):
        return pltpu.make_async_remote_copy(
            src_ref=piece_out.at[q],
            dst_ref=piece_in.at[r],
            send_sem=piece_send.at[q, col],
            recv_sem=piece_recv.at[r],
            device_id=(g, c * per + q, col),
            device_id_type=MESH,
        )

    def each_piece(act):
        for q in range(per):
            for col in range(2):

                @pl.when((c * per + q != r) | (col != c))
                def _():
                    act(piece_copy(q, col))

    each_piece(start)

    @pl.when(r // per == c)
    def _():
        piece_in[r] = piece_out[r % per]

    gate_ref[...] = jax.nn.sigmoid(project(normed, 1, 4, 1))
    tri[...] = jnp.zeros_like(tri)

    def incoming_block(row):
        @pl.when((row != r) | (r // per != c))
        def _():
            pltpu.make_async_remote_copy(
                src_ref=piece_in.at[row],
                dst_ref=piece_in.at[row],
                send_sem=piece_send.at[0, 0],
                recv_sem=piece_recv.at[row],
                device_id=other,
                device_id_type=MESH,
            ).wait_recv()

        piece_f32[0] = piece_in[row].astype(F32)
        for i0 in range(0, ri, ri // 2):
            sums = [tri[i0 + i] for i in range(ri // 2)]
            for kk in range(ri):
                right = slots1[row, kk * ci : (kk + 1) * ci, :].astype(F32)
                for i in range(ri // 2):
                    at = kk * ri + i0 + i
                    sums[i] = sums[i] + right * piece_f32[0, at : at + 1, :]
            for i in range(ri // 2):
                tri[i0 + i] = sums[i]

    gather(1, slots1, incoming_block)
    out_ref[...] = finish_update(1, out_ref[...])

    half_copy.wait_send()
    finish_sends(0, slots0)
    finish_sends(1, slots1)
    each_piece(end)


def kernel_body(n_row, pair, chain, in_gain, in_proj, out_gain, out_proj):
    ri, ci, _ = pair.shape
    cells = ri * ci
    piece = -(-ri * ri // 16) * 16
    per = ci // ri
    cuts = (0, (ri // 2 // 2) * 2 * ci, cells)
    n_cut = len(cuts) - 1
    vmem = pl.BlockSpec(memory_space=pltpu.VMEM)
    out = pl.pallas_call(
        functools.partial(kernel, n_row, ri, ci, cuts),
        out_shape=jax.ShapeDtypeStruct((cells, C), BF16),
        in_specs=[vmem] * 6,
        out_specs=vmem,
        scratch_shapes=[
            pltpu.VMEM((n_row, cells, CH), BF16),
            pltpu.VMEM((n_row, cells, CH), BF16),
            pltpu.VMEM((per, piece, CH), BF16),
            pltpu.VMEM((n_row, piece, CH), BF16),
            pltpu.VMEM((per, piece, CH), F32),
            pltpu.VMEM((ri, ci, CH), F32),
            pltpu.VMEM((n_row, ri, ri, CH), F32),
            pltpu.VMEM((ri, ci, CH), F32),
            pltpu.VMEM((cells, CH), BF16),
            pltpu.VMEM((cells, CH), BF16),
            pltpu.VMEM((cells, C), F32),
            pltpu.VMEM((cells, 1), F32),
            pltpu.SemaphoreType.DMA((2, 3, n_row, n_cut)),
            pltpu.SemaphoreType.DMA((2, n_row, n_cut)),
            pltpu.SemaphoreType.DMA((per, 2)),
            pltpu.SemaphoreType.DMA((n_row,)),
            pltpu.SemaphoreType.DMA,
            pltpu.SemaphoreType.DMA,
        ],
        compiler_params=pltpu.CompilerParams(
            collective_id=0, has_side_effects=True, vmem_limit_bytes=32 * 1024 * 1024
        ),
    )(pair.reshape(cells, C), chain.reshape(1, -1), in_gain, in_proj, out_gain, out_proj)
    return out.reshape(ri, ci, C)


def solution(mesh):
    n_row, n_col = mesh.shape["row"], mesh.shape["col"]
    small = n_col == 2 and n_row == 8
    return jax.shard_map(
        functools.partial(kernel_body, n_row) if small else body,
        mesh=mesh,
        in_specs=(P(("groups", "row"), "col", None), P("groups"), P(), P(), P(), P()),
        out_specs=P(("groups", "row"), "col", None),
        check_vma=False,
    )
```

```python
import functools

import jax
import jax.numpy as jnp
from jax import lax
from jax.experimental import pallas as pl
from jax.experimental.pallas import tpu as pltpu
from jax.sharding import PartitionSpec as P

C = 128
CH = 128
F32 = jnp.float32
BF16 = jnp.bfloat16
MESH = pl.DeviceIdType.MESH


def normalize(values, gain):
    mean = jnp.mean(values, axis=-1, keepdims=True)
    centered = values - mean
    spread = jnp.mean(centered * centered, axis=-1, keepdims=True)
    return centered * lax.rsqrt(spread + 1e-05) * gain


def branch_terms(tile, rows_valid, cols_valid, gain, weights):
    normed = normalize(tile.astype(jnp.float32), gain).astype(jnp.bfloat16)
    flat = normed.reshape(-1, normed.shape[-1])
    proj = jnp.dot(flat, weights, preferred_element_type=jnp.float32)
    proj = proj.reshape(tile.shape[0], tile.shape[1], -1)
    mask = (rows_valid[:, None] * cols_valid[None, :])[:, :, None]
    left = (jax.nn.sigmoid(proj[..., 0:CH]) * proj[..., CH : 2 * CH] * mask).astype(jnp.bfloat16)
    right = (jax.nn.sigmoid(proj[..., 2 * CH : 3 * CH]) * proj[..., 3 * CH : 4 * CH] * mask).astype(
        jnp.bfloat16
    )
    gate = jax.nn.sigmoid(proj[..., 4 * CH : 4 * CH + C])
    return (left, right, gate)


def finish(tile, tri, gate, tri_gain, out_weights):
    tri_normed = normalize(tri, tri_gain).astype(jnp.bfloat16)
    projected = jnp.dot(
        tri_normed.reshape(-1, tri.shape[-1]), out_weights, preferred_element_type=jnp.float32
    )
    update = gate * projected.reshape(gate.shape)
    return (tile.astype(jnp.float32) + update).astype(jnp.bfloat16)


def outgoing(tile, rows_valid, cols_valid, gain, weights, tri_gain, out_weights):
    left, right, gate = branch_terms(tile, rows_valid, cols_valid, gain, weights)
    right_cols = lax.all_gather(right, "row", axis=0, tiled=True)
    right_rows = lax.all_to_all(right_cols, "col", split_axis=0, concat_axis=1, tiled=True)
    tri = jnp.einsum(
        "ikc,jkc->ijc",
        lax.all_gather(left, "col", axis=1, tiled=True),
        right_rows,
        preferred_element_type=jnp.float32,
    )
    return finish(tile, tri, gate, tri_gain, out_weights)


def incoming(tile, rows_valid, cols_valid, gain, weights, tri_gain, out_weights):
    left, right, gate = branch_terms(tile, rows_valid, cols_valid, gain, weights)
    strip = lax.all_gather(left, "col", axis=1, tiled=True)
    left_cols = lax.all_to_all(strip, "row", split_axis=1, concat_axis=0, tiled=True)
    tri = jnp.einsum(
        "kic,kjc->ijc",
        left_cols,
        lax.all_gather(right, "row", axis=0, tiled=True),
        preferred_element_type=jnp.float32,
    )
    return finish(tile, tri, gate, tri_gain, out_weights)


def body(pair, chain, in_gain, in_proj, out_gain, out_proj):
    row_count = pair.shape[0]
    col_count = pair.shape[1]
    valid = (chain >= 0).astype(jnp.float32)
    rows_valid = lax.dynamic_slice_in_dim(valid, lax.axis_index("row") * row_count, row_count, 0)
    cols_valid = lax.dynamic_slice_in_dim(valid, lax.axis_index("col") * col_count, col_count, 0)
    pair_mid = outgoing(
        pair, rows_valid, cols_valid, in_gain[0], in_proj[0], out_gain[0], out_proj[0]
    )
    return incoming(
        pair_mid, rows_valid, cols_valid, in_gain[1], in_proj[1], out_gain[1], out_proj[1]
    )


def layer_norm(values, gain):
    mean = jnp.mean(values, axis=-1, keepdims=True)
    centered = values - mean
    spread = jnp.mean(centered * centered, axis=-1, keepdims=True)
    return (centered * lax.rsqrt(spread + 1e-05) * gain).astype(BF16)


def kernel(
    n_row,
    ri,
    ci,
    cuts,
    pair_hbm,
    chain_hbm,
    in_gain_hbm,
    in_proj_hbm,
    out_gain_hbm,
    out_proj_hbm,
    out_ref,
    pair_ref,
    chain_ref,
    in_gain,
    in_proj,
    out_gain,
    out_proj,
    load_sem,
    slots0,
    slots1,
    piece_out,
    piece_in,
    piece_f32,
    left_f32,
    acc,
    tri,
    half_out,
    half_in,
    gate_ref,
    mask_ref,
    send_sem,
    recv_sem,
    piece_send,
    piece_recv,
    half_send,
    half_recv,
    part_out,
    part_in,
    part_send,
    part_recv,
):
    g = lax.axis_index("groups")
    r = lax.axis_index("row")
    c = lax.axis_index("col")
    n_z = n_row // 2
    per = ci // ri
    z = r // 2
    k = r % 2
    cells = ri * ci

    barrier = pltpu.get_barrier_semaphore()
    for dr in range(n_row):
        for dc in range(2):
            if dr or dc:
                pl.semaphore_signal(
                    barrier,
                    inc=1,
                    device_id=(g, lax.rem(r + dr, n_row), lax.rem(c + dc, 2)),
                    device_id_type=MESH,
                )

    sources = (
        (pair_hbm, pair_ref),
        (in_gain_hbm, in_gain),
        (in_proj_hbm, in_proj),
        (chain_hbm, chain_ref),
        (out_gain_hbm, out_gain),
        (out_proj_hbm, out_proj),
    )
    loads = [
        pltpu.make_async_copy(src, dst, load_sem.at[at]) for at, (src, dst) in enumerate(sources)
    ]
    for load in loads:
        load.start()
    for load in loads:
        load.wait()

    shape = (ri, ci, n_row * ri)
    lane = lax.broadcasted_iota(jnp.int32, shape, 2)
    row_at = lax.broadcasted_iota(jnp.int32, shape, 0) + r * ri
    col_at = lax.broadcasted_iota(jnp.int32, shape, 1) + c * ci
    padding = jnp.where(chain_ref[...] < 0, 1.0, 0.0).astype(F32).reshape(1, 1, -1)
    hit = jnp.where((lane == row_at) | (lane == col_at), padding, 0.0)
    mask_ref[...] = 1.0 - jnp.max(hit.reshape(cells, -1), axis=-1, keepdims=True)

    def project(normed, u, first, count):
        return jnp.dot(
            normed,
            in_proj[u, :, first * CH : (first + count) * CH],
            preferred_element_type=F32,
        )

    def gated(both):
        return jax.nn.sigmoid(both[:, :CH]) * both[:, CH:] * mask_ref[...]

    def gather_copy(u, slots, row, cut, way, target):
        lo, hi = cuts[cut], cuts[cut + 1]
        part = slots.at[row, pl.ds(lo, hi - lo)]
        return pltpu.make_async_remote_copy(
            src_ref=part,
            dst_ref=part,
            send_sem=send_sem.at[u, way, row, cut],
            recv_sem=recv_sem.at[u, row, cut],
            device_id=target,
            device_id_type=MESH,
        )

    n_cut = len(cuts) - 1
    up = (g, lax.rem(r + 2, n_row), c)
    down = (g, lax.rem(r + n_row - 2, n_row), c)
    other = (g, r + 1 - 2 * k, c)

    half = r // per
    beside = (g, r + 2 - 4 * (z % 2), c)

    def forward(u, slots, row, cut, goes_up, goes_down, act):
        @pl.when(goes_up)
        def _():
            act(gather_copy(u, slots, row, cut, 0, up))

        @pl.when(goes_down)
        def _():
            act(gather_copy(u, slots, row, cut, 1, down))

        act(gather_copy(u, slots, row, cut, 2, other))

    def each_arrival(visit):
        for dist in range(1, n_z):

            @pl.when(z >= dist)
            def _():
                visit(z - dist, 0)

            @pl.when(z + dist < n_z)
            def _():
                visit(z + dist, 1)

    def start(copy):
        copy.start()

    def end(copy):
        copy.wait_send()

    def send_own(u, slots):
        for cut in range(n_cut):
            forward(u, slots, r, cut, z < n_z - 1, z > 0, start)

    def gather(u, slots, work, lag):
        def pass_on(dist):
            for cut in range(n_cut):

                @pl.when(z >= dist)
                def _():
                    mine = 2 * (z - dist) + k
                    gather_copy(u, slots, mine, cut, 0, other).wait_recv()
                    forward(u, slots, mine, cut, z < n_z - 1, False, start)

                @pl.when(z + dist < n_z)
                def _():
                    mine = 2 * (z + dist) + k
                    gather_copy(u, slots, mine, cut, 0, other).wait_recv()
                    forward(u, slots, mine, cut, False, z > 0, start)

        def work_at(z_from):
            work(2 * z_from + k)
            theirs = 2 * z_from + 1 - k
            for cut in range(n_cut):
                gather_copy(u, slots, theirs, cut, 2, other).wait_recv()
            work(theirs)

        def work_dist(dist):
            if dist == 0:
                work_at(z)
                return

            @pl.when(z >= dist)
            def _():
                work_at(z - dist)

            @pl.when(z + dist < n_z)
            def _():
                work_at(z + dist)

        for dist in range(n_z):
            if dist:
                pass_on(dist)
            if dist >= lag:
                work_dist(dist - lag)
        for dist in range(n_z - lag, n_z):
            work_dist(dist)

    def finish_sends(u, slots):
        for cut in range(n_cut):
            forward(u, slots, r, cut, z < n_z - 1, z > 0, end)

        def visit(z_from, side):
            for cut in range(n_cut):
                if side == 0:
                    forward(u, slots, 2 * z_from + k, cut, z < n_z - 1, False, end)
                else:
                    forward(u, slots, 2 * z_from + k, cut, False, z > 0, end)

        each_arrival(visit)

    def finish_update(u, tile):
        normed = layer_norm(tri[...].reshape(cells, CH), out_gain[u : u + 1, :])
        projected = jnp.dot(normed, out_proj[u], preferred_element_type=F32)
        return (tile.astype(F32) + gate_ref[...] * projected).astype(BF16)

    normed = layer_norm(pair_ref[...].astype(F32), in_gain[0:1, :])
    slots0[r] = gated(project(normed, 0, 2, 2)).astype(BF16)
    pl.semaphore_wait(barrier, 2 * n_row - 1)
    send_own(0, slots0)
    left_f32[...] = gated(project(normed, 0, 0, 2)).astype(BF16).astype(F32).reshape(ri, ci, CH)
    gate_ref[...] = jax.nn.sigmoid(project(normed, 0, 4, 1))

    def half_copy(q):
        return pltpu.make_async_remote_copy(
            src_ref=half_out.at[q],
            dst_ref=half_in.at[q],
            send_sem=half_send.at[q],
            recv_sem=half_recv.at[q],
            device_id=(g, r, 1 - c),
            device_id_type=MESH,
        )

    def outgoing_block(row):
        block = slots0[row].astype(F32).reshape(ri, ci, CH)
        for i in range(ri):
            acc[row, i * ri : (i + 1) * ri, :] = jnp.sum(left_f32[i][None] * block, axis=1)

        @pl.when(row // per != c)
        def _():
            q = row % per
            half_out[q] = acc[row].astype(BF16)
            half_copy(q).start()

    gather(0, slots0, outgoing_block, 0)
    for q in range(per):
        half_copy(q).wait_recv()
        piece_f32[q] = acc[c * per + q] + half_in[q].astype(F32)
        for i in range(ri):
            tri[i, q * ri : (q + 1) * ri, :] = piece_f32[q, i * ri : (i + 1) * ri, :]
    mid = finish_update(0, pair_ref[...])
    out_ref[...] = mid

    normed = layer_norm(mid.astype(F32), in_gain[1:2, :])
    slots1[r] = gated(project(normed, 1, 2, 2)).astype(BF16)
    for cut in range(n_cut):
        gather_copy(1, slots1, r, cut, 0, beside).start()
        gather_copy(1, slots1, r, cut, 2, other).start()
    left_f32[...] = gated(project(normed, 1, 0, 2)).reshape(ri, ci, CH)
    for q in range(per):
        for kk in range(ri):
            piece_f32[q, kk * ri : (kk + 1) * ri, :] = left_f32[kk, q * ri : (q + 1) * ri, :]
        piece_out[q, :, :] = piece_f32[q].astype(BF16)

    def piece_copy(at, col):
        q = lax.rem(at + 2 * (1 - z % 2), per)
        return pltpu.make_async_remote_copy(
            src_ref=piece_out.at[q],
            dst_ref=piece_in.at[c * per + r % per],
            send_sem=piece_send.at[q, col],
            recv_sem=piece_recv.at[c * per + r % per],
            device_id=(g, half * per + q, col),
            device_id_type=MESH,
        )

    def each_piece(act):
        for at in range(per):
            for col in range(2):
                mine = (lax.rem(at + 2 * (1 - z % 2), per) == r % per) & (c == col)

                @pl.when(jnp.logical_not(mine))
                def _():
                    act(piece_copy(at, col))

    each_piece(start)
    piece_in[c * per + r % per] = piece_out[r % per]
    gate_ref[...] = jax.nn.sigmoid(project(normed, 1, 4, 1))

    theirs = r + 2 - 4 * (z % 2)
    for cut in range(n_cut):
        gather_copy(1, slots1, theirs, cut, 0, beside).wait_recv()
        gather_copy(1, slots1, theirs, cut, 2, other).start()

    def wait_pieces(owner):
        for s in range(per):
            slot = owner * per + s

            @pl.when(slot != c * per + r % per)
            def _():
                pltpu.make_async_remote_copy(
                    src_ref=piece_in.at[slot],
                    dst_ref=piece_in.at[slot],
                    send_sem=piece_send.at[0, 0],
                    recv_sem=piece_recv.at[slot],
                    device_id=other,
                    device_id_type=MESH,
                ).wait_recv()

        for s in range(per):
            piece_f32[s] = piece_in[owner * per + s].astype(F32)

    def partial_sums(lo, hi):
        sums = [jnp.zeros((ci, CH), F32) for _ in range(lo, hi)]
        for s in range(per):
            for kk in range(ri):
                right = slots1[half * per + s, kk * ci : (kk + 1) * ci, :].astype(F32)
                for i in range(lo, hi):
                    at = kk * ri + i
                    sums[i - lo] = sums[i - lo] + right * piece_f32[s, at : at + 1, :]
        return sums

    def partial_copy(cut):
        lo, hi = cuts[cut], cuts[cut + 1]
        return pltpu.make_async_remote_copy(
            src_ref=part_out.at[pl.ds(lo, hi - lo)],
            dst_ref=part_in.at[pl.ds(lo, hi - lo)],
            send_sem=part_send.at[cut],
            recv_sem=part_recv.at[cut],
            device_id=(g, (1 - half) * per + r % per, c),
            device_id_type=MESH,
        )

    wait_pieces(1 - half)
    for cut in range(n_cut):
        gather_copy(1, slots1, r + 1 - 2 * k, cut, 2, other).wait_recv()
        gather_copy(1, slots1, theirs + 1 - 2 * k, cut, 2, other).wait_recv()
    for cut in range(n_cut):
        lo, hi = cuts[cut] // ci, cuts[cut + 1] // ci
        sums = partial_sums(lo, hi)
        for i in range(lo, hi):
            part_out[i * ci : (i + 1) * ci, :] = sums[i - lo].astype(BF16)
        partial_copy(cut).start()

    wait_pieces(half)
    for cut in range(n_cut):
        lo, hi = cuts[cut] // ci, cuts[cut + 1] // ci
        sums = partial_sums(lo, hi)
        for i in range(lo, hi):
            tri[i] = sums[i - lo]
    for cut in range(n_cut):
        partial_copy(cut).wait_recv()
    tri[...] = tri[...] + part_in[...].astype(F32).reshape(ri, ci, CH)
    out_ref[...] = finish_update(1, out_ref[...])

    for q in range(per):
        half_copy(q).wait_send()
    finish_sends(0, slots0)
    for cut in range(n_cut):
        gather_copy(1, slots1, r, cut, 0, beside).wait_send()
        gather_copy(1, slots1, r, cut, 2, other).wait_send()
        gather_copy(1, slots1, theirs, cut, 2, other).wait_send()
        partial_copy(cut).wait_send()
    each_piece(end)


def kernel_body(n_row, pair, chain, in_gain, in_proj, out_gain, out_proj):
    ri, ci, _ = pair.shape
    cells = ri * ci
    piece = -(-ri * ri // 16) * 16
    per = ci // ri
    cuts = (0, (ri // 2 // 2) * 2 * ci, cells)
    n_cut = len(cuts) - 1
    vmem = pl.BlockSpec(memory_space=pltpu.VMEM)
    out = pl.pallas_call(
        functools.partial(kernel, n_row, ri, ci, cuts),
        out_shape=jax.ShapeDtypeStruct((cells, C), BF16),
        in_specs=[pl.BlockSpec(memory_space=pltpu.HBM)] * 6,
        out_specs=vmem,
        scratch_shapes=[
            pltpu.VMEM((cells, C), BF16),
            pltpu.VMEM((1, n_row * ri), jnp.int32),
            pltpu.VMEM(in_gain.shape, F32),
            pltpu.VMEM(in_proj.shape, BF16),
            pltpu.VMEM(out_gain.shape, F32),
            pltpu.VMEM(out_proj.shape, BF16),
            pltpu.SemaphoreType.DMA((6,)),
            pltpu.VMEM((n_row, cells, CH), BF16),
            pltpu.VMEM((n_row, cells, CH), BF16),
            pltpu.VMEM((per, piece, CH), BF16),
            pltpu.VMEM((n_row, piece, CH), BF16),
            pltpu.VMEM((per, piece, CH), F32),
            pltpu.VMEM((ri, ci, CH), F32),
            pltpu.VMEM((n_row, piece, CH), F32),
            pltpu.VMEM((ri, ci, CH), F32),
            pltpu.VMEM((per, piece, CH), BF16),
            pltpu.VMEM((per, piece, CH), BF16),
            pltpu.VMEM((cells, C), F32),
            pltpu.VMEM((cells, 1), F32),
            pltpu.SemaphoreType.DMA((2, 3, n_row, n_cut)),
            pltpu.SemaphoreType.DMA((2, n_row, n_cut)),
            pltpu.SemaphoreType.DMA((per, 2)),
            pltpu.SemaphoreType.DMA((n_row,)),
            pltpu.SemaphoreType.DMA((per,)),
            pltpu.SemaphoreType.DMA((per,)),
            pltpu.VMEM((cells, CH), BF16),
            pltpu.VMEM((cells, CH), BF16),
            pltpu.SemaphoreType.DMA((n_cut,)),
            pltpu.SemaphoreType.DMA((n_cut,)),
        ],
        compiler_params=pltpu.CompilerParams(
            collective_id=0, has_side_effects=True, vmem_limit_bytes=60 * 1024 * 1024
        ),
    )(pair.reshape(cells, C), chain.reshape(1, -1), in_gain, in_proj, out_gain, out_proj)
    return out.reshape(ri, ci, C)


def solution(mesh):
    n_row, n_col = mesh.shape["row"], mesh.shape["col"]
    small = n_col == 2 and n_row == 8
    return jax.shard_map(
        functools.partial(kernel_body, n_row) if small else body,
        mesh=mesh,
        in_specs=(P(("groups", "row"), "col", None), P("groups"), P(), P(), P(), P()),
        out_specs=P(("groups", "row"), "col", None),
        check_vma=False,
    )
```

```python
import functools

import jax
import jax.numpy as jnp
from jax import lax
from jax.experimental import pallas as pl
from jax.experimental.pallas import tpu as pltpu
from jax.sharding import PartitionSpec as P

C = 128
CH = 128
F32 = jnp.float32
BF16 = jnp.bfloat16
MESH = pl.DeviceIdType.MESH


def normalize(values, gain):
    mean = jnp.mean(values, axis=-1, keepdims=True)
    centered = values - mean
    spread = jnp.mean(centered * centered, axis=-1, keepdims=True)
    return centered * lax.rsqrt(spread + 1e-05) * gain


def branch_terms(tile, rows_valid, cols_valid, gain, weights):
    normed = normalize(tile.astype(jnp.float32), gain).astype(jnp.bfloat16)
    flat = normed.reshape(-1, normed.shape[-1])
    proj = jnp.dot(flat, weights, preferred_element_type=jnp.float32)
    proj = proj.reshape(tile.shape[0], tile.shape[1], -1)
    mask = (rows_valid[:, None] * cols_valid[None, :])[:, :, None]
    left = (jax.nn.sigmoid(proj[..., 0:CH]) * proj[..., CH : 2 * CH] * mask).astype(jnp.bfloat16)
    right = (jax.nn.sigmoid(proj[..., 2 * CH : 3 * CH]) * proj[..., 3 * CH : 4 * CH] * mask).astype(
        jnp.bfloat16
    )
    gate = jax.nn.sigmoid(proj[..., 4 * CH : 4 * CH + C])
    return (left, right, gate)


def finish(tile, tri, gate, tri_gain, out_weights):
    tri_normed = normalize(tri, tri_gain).astype(jnp.bfloat16)
    projected = jnp.dot(
        tri_normed.reshape(-1, tri.shape[-1]), out_weights, preferred_element_type=jnp.float32
    )
    update = gate * projected.reshape(gate.shape)
    return (tile.astype(jnp.float32) + update).astype(jnp.bfloat16)


def outgoing(tile, rows_valid, cols_valid, gain, weights, tri_gain, out_weights):
    left, right, gate = branch_terms(tile, rows_valid, cols_valid, gain, weights)
    right_cols = lax.all_gather(right, "row", axis=0, tiled=True)
    right_rows = lax.all_to_all(right_cols, "col", split_axis=0, concat_axis=1, tiled=True)
    tri = jnp.einsum(
        "ikc,jkc->ijc",
        lax.all_gather(left, "col", axis=1, tiled=True),
        right_rows,
        preferred_element_type=jnp.float32,
    )
    return finish(tile, tri, gate, tri_gain, out_weights)


def incoming(tile, rows_valid, cols_valid, gain, weights, tri_gain, out_weights):
    left, right, gate = branch_terms(tile, rows_valid, cols_valid, gain, weights)
    strip = lax.all_gather(left, "col", axis=1, tiled=True)
    left_cols = lax.all_to_all(strip, "row", split_axis=1, concat_axis=0, tiled=True)
    tri = jnp.einsum(
        "kic,kjc->ijc",
        left_cols,
        lax.all_gather(right, "row", axis=0, tiled=True),
        preferred_element_type=jnp.float32,
    )
    return finish(tile, tri, gate, tri_gain, out_weights)


def body(pair, chain, in_gain, in_proj, out_gain, out_proj):
    row_count = pair.shape[0]
    col_count = pair.shape[1]
    valid = (chain >= 0).astype(jnp.float32)
    rows_valid = lax.dynamic_slice_in_dim(valid, lax.axis_index("row") * row_count, row_count, 0)
    cols_valid = lax.dynamic_slice_in_dim(valid, lax.axis_index("col") * col_count, col_count, 0)
    pair_mid = outgoing(
        pair, rows_valid, cols_valid, in_gain[0], in_proj[0], out_gain[0], out_proj[0]
    )
    return incoming(
        pair_mid, rows_valid, cols_valid, in_gain[1], in_proj[1], out_gain[1], out_proj[1]
    )


def layer_norm(values, gain):
    mean = jnp.mean(values, axis=-1, keepdims=True)
    centered = values - mean
    spread = jnp.mean(centered * centered, axis=-1, keepdims=True)
    return (centered * lax.rsqrt(spread + 1e-05) * gain).astype(BF16)


def kernel(
    n_row,
    ri,
    ci,
    cuts,
    pair_hbm,
    chain_hbm,
    in_gain_hbm,
    in_proj_hbm,
    out_gain_hbm,
    out_proj_hbm,
    out_ref,
    pair_ref,
    chain_ref,
    in_gain,
    in_proj,
    out_gain,
    out_proj,
    load_sem,
    slots0,
    slots1,
    piece_out,
    piece_in,
    piece_f32,
    left_f32,
    acc,
    tri,
    half_out,
    half_in,
    gate_ref,
    mask_ref,
    send_sem,
    recv_sem,
    piece_send,
    piece_recv,
    half_send,
    half_recv,
    part_out,
    part_in,
    part_send,
    part_recv,
):
    g = lax.axis_index("groups")
    r = lax.axis_index("row")
    c = lax.axis_index("col")
    n_z = n_row // 2
    per = ci // ri
    z = r // 2
    k = r % 2
    cells = ri * ci

    half = r // per
    inner = (z > 0) & (z < n_z - 1)
    counterpart = (g, (1 - half) * per + r % per, c)
    across = (g, lax.rem(r + 2 - 4 * half + n_row, n_row), c)
    barrier = pltpu.get_barrier_semaphore()

    def greet(target):
        pl.semaphore_signal(barrier, inc=1, device_id=target, device_id_type=MESH)

    @pl.when(inner)
    def _():
        greet(across)

    greet(counterpart)
    for dr in range(per):
        for dc in range(2):
            if dr or dc:
                greet((g, half * per + lax.rem(r + dr, per), lax.rem(c + dc, 2)))

    sources = (
        (pair_hbm, pair_ref),
        (in_gain_hbm, in_gain),
        (in_proj_hbm, in_proj),
        (chain_hbm, chain_ref),
        (out_gain_hbm, out_gain),
        (out_proj_hbm, out_proj),
    )
    loads = [
        pltpu.make_async_copy(src, dst, load_sem.at[at]) for at, (src, dst) in enumerate(sources)
    ]
    for load in loads:
        load.start()
    for load in loads:
        load.wait()

    shape = (ri, ci, n_row * ri)
    lane = lax.broadcasted_iota(jnp.int32, shape, 2)
    row_at = lax.broadcasted_iota(jnp.int32, shape, 0) + r * ri
    col_at = lax.broadcasted_iota(jnp.int32, shape, 1) + c * ci
    padding = jnp.where(chain_ref[...] < 0, 1.0, 0.0).astype(F32).reshape(1, 1, -1)
    hit = jnp.where((lane == row_at) | (lane == col_at), padding, 0.0)
    mask_ref[...] = 1.0 - jnp.max(hit.reshape(cells, -1), axis=-1, keepdims=True)

    def project(normed, u, first, count):
        return jnp.dot(
            normed,
            in_proj[u, :, first * CH : (first + count) * CH],
            preferred_element_type=F32,
        )

    def gated(both):
        return jax.nn.sigmoid(both[:, :CH]) * both[:, CH:] * mask_ref[...]

    def gather_copy(u, slots, row, cut, way, target):
        lo, hi = cuts[cut], cuts[cut + 1]
        part = slots.at[row, pl.ds(lo, hi - lo)]
        return pltpu.make_async_remote_copy(
            src_ref=part,
            dst_ref=part,
            send_sem=send_sem.at[u, way, row, cut],
            recv_sem=recv_sem.at[u, row, cut],
            device_id=target,
            device_id_type=MESH,
        )

    n_cut = len(cuts) - 1
    up = (g, lax.rem(r + 2, n_row), c)
    down = (g, lax.rem(r + n_row - 2, n_row), c)
    other = (g, r + 1 - 2 * k, c)

    beside = (g, r + 2 - 4 * (z % 2), c)

    def forward(u, slots, row, cut, goes_up, goes_down, act):
        @pl.when(goes_up)
        def _():
            act(gather_copy(u, slots, row, cut, 0, up))

        @pl.when(goes_down)
        def _():
            act(gather_copy(u, slots, row, cut, 1, down))

        act(gather_copy(u, slots, row, cut, 2, other))

    def each_arrival(visit):
        for dist in range(1, n_z):

            @pl.when(z >= dist)
            def _():
                visit(z - dist, 0)

            @pl.when(z + dist < n_z)
            def _():
                visit(z + dist, 1)

    def start(copy):
        copy.start()

    def end(copy):
        copy.wait_send()

    def send_own(u, slots):
        for cut in range(n_cut):
            forward(u, slots, r, cut, z < n_z - 1, z > 0, start)

    def gather(u, slots, work, lag):
        def pass_on(dist):
            for cut in range(n_cut):

                @pl.when(z >= dist)
                def _():
                    mine = 2 * (z - dist) + k
                    gather_copy(u, slots, mine, cut, 0, other).wait_recv()
                    forward(u, slots, mine, cut, z < n_z - 1, False, start)

                @pl.when(z + dist < n_z)
                def _():
                    mine = 2 * (z + dist) + k
                    gather_copy(u, slots, mine, cut, 0, other).wait_recv()
                    forward(u, slots, mine, cut, False, z > 0, start)

        def work_at(z_from):
            work(2 * z_from + k)
            theirs = 2 * z_from + 1 - k
            for cut in range(n_cut):
                gather_copy(u, slots, theirs, cut, 2, other).wait_recv()
            work(theirs)

        def work_dist(dist):
            if dist == 0:
                work_at(z)
                return

            @pl.when(z >= dist)
            def _():
                work_at(z - dist)

            @pl.when(z + dist < n_z)
            def _():
                work_at(z + dist)

        for dist in range(n_z):
            if dist:
                pass_on(dist)
            if dist >= lag:
                work_dist(dist - lag)
        for dist in range(n_z - lag, n_z):
            work_dist(dist)

    def finish_sends(u, slots):
        for cut in range(n_cut):
            forward(u, slots, r, cut, z < n_z - 1, z > 0, end)

        def visit(z_from, side):
            for cut in range(n_cut):
                if side == 0:
                    forward(u, slots, 2 * z_from + k, cut, z < n_z - 1, False, end)
                else:
                    forward(u, slots, 2 * z_from + k, cut, False, z > 0, end)

        each_arrival(visit)

    def finish_update(u, tile):
        normed = layer_norm(tri[...].reshape(cells, CH), out_gain[u : u + 1, :])
        projected = jnp.dot(normed, out_proj[u], preferred_element_type=F32)
        return (tile.astype(F32) + gate_ref[...] * projected).astype(BF16)

    normed = layer_norm(pair_ref[...].astype(F32), in_gain[0:1, :])
    slots0[r] = gated(project(normed, 0, 2, 2)).astype(BF16)

    @pl.when(inner)
    def _():
        pl.semaphore_wait(barrier, 2 * per + 1)

    @pl.when(jnp.logical_not(inner))
    def _():
        pl.semaphore_wait(barrier, 2 * per)

    send_own(0, slots0)
    left_f32[...] = gated(project(normed, 0, 0, 2)).astype(BF16).astype(F32).reshape(ri, ci, CH)
    gate_ref[...] = jax.nn.sigmoid(project(normed, 0, 4, 1))

    def half_copy(q):
        return pltpu.make_async_remote_copy(
            src_ref=half_out.at[q],
            dst_ref=half_in.at[q],
            send_sem=half_send.at[q],
            recv_sem=half_recv.at[q],
            device_id=(g, r, 1 - c),
            device_id_type=MESH,
        )

    def outgoing_block(row):
        block = slots0[row].astype(F32).reshape(ri, ci, CH)
        for i in range(ri):
            acc[row, i * ri : (i + 1) * ri, :] = jnp.sum(left_f32[i][None] * block, axis=1)

        @pl.when(row // per != c)
        def _():
            q = row % per
            half_out[q] = acc[row].astype(BF16)
            half_copy(q).start()

    gather(0, slots0, outgoing_block, 0)
    for q in range(per):
        half_copy(q).wait_recv()
        piece_f32[q] = acc[c * per + q] + half_in[q].astype(F32)
        for i in range(ri):
            tri[i, q * ri : (q + 1) * ri, :] = piece_f32[q, i * ri : (i + 1) * ri, :]
    mid = finish_update(0, pair_ref[...])
    out_ref[...] = mid

    normed = layer_norm(mid.astype(F32), in_gain[1:2, :])
    slots1[r] = gated(project(normed, 1, 2, 2)).astype(BF16)
    for cut in range(n_cut):
        gather_copy(1, slots1, r, cut, 0, beside).start()
        gather_copy(1, slots1, r, cut, 2, other).start()
    left_f32[...] = gated(project(normed, 1, 0, 2)).reshape(ri, ci, CH)
    for q in range(per):
        for kk in range(ri):
            piece_f32[q, kk * ri : (kk + 1) * ri, :] = left_f32[kk, q * ri : (q + 1) * ri, :]
        piece_out[q, :, :] = piece_f32[q].astype(BF16)

    def piece_copy(at, col):
        q = lax.rem(at + 2 * (1 - z % 2), per)
        return pltpu.make_async_remote_copy(
            src_ref=piece_out.at[q],
            dst_ref=piece_in.at[c * per + r % per],
            send_sem=piece_send.at[q, col],
            recv_sem=piece_recv.at[c * per + r % per],
            device_id=(g, half * per + q, col),
            device_id_type=MESH,
        )

    def each_piece(act):
        for at in range(per):
            for col in range(2):
                mine = (lax.rem(at + 2 * (1 - z % 2), per) == r % per) & (c == col)

                @pl.when(jnp.logical_not(mine))
                def _():
                    act(piece_copy(at, col))

    each_piece(start)
    piece_in[c * per + r % per] = piece_out[r % per]
    gate_ref[...] = jax.nn.sigmoid(project(normed, 1, 4, 1))

    theirs = r + 2 - 4 * (z % 2)
    for cut in range(n_cut):
        gather_copy(1, slots1, theirs, cut, 0, beside).wait_recv()
        gather_copy(1, slots1, theirs, cut, 2, other).start()

    def wait_pieces(owner):
        for s in range(per):
            slot = owner * per + s

            @pl.when(slot != c * per + r % per)
            def _():
                pltpu.make_async_remote_copy(
                    src_ref=piece_in.at[slot],
                    dst_ref=piece_in.at[slot],
                    send_sem=piece_send.at[0, 0],
                    recv_sem=piece_recv.at[slot],
                    device_id=other,
                    device_id_type=MESH,
                ).wait_recv()

        for s in range(per):
            piece_f32[s] = piece_in[owner * per + s].astype(F32)

    def partial_sums(lo, hi):
        sums = [jnp.zeros((ci, CH), F32) for _ in range(lo, hi)]
        for s in range(per):
            for kk in range(ri):
                right = slots1[half * per + s, kk * ci : (kk + 1) * ci, :].astype(F32)
                for i in range(lo, hi):
                    at = kk * ri + i
                    sums[i - lo] = sums[i - lo] + right * piece_f32[s, at : at + 1, :]
        return sums

    def partial_copy(cut):
        lo, hi = cuts[cut], cuts[cut + 1]
        return pltpu.make_async_remote_copy(
            src_ref=part_out.at[pl.ds(lo, hi - lo)],
            dst_ref=part_in.at[pl.ds(lo, hi - lo)],
            send_sem=part_send.at[cut],
            recv_sem=part_recv.at[cut],
            device_id=counterpart,
            device_id_type=MESH,
        )

    wait_pieces(1 - half)
    for cut in range(n_cut):
        gather_copy(1, slots1, r + 1 - 2 * k, cut, 2, other).wait_recv()
        gather_copy(1, slots1, theirs + 1 - 2 * k, cut, 2, other).wait_recv()
    for cut in range(n_cut):
        lo, hi = cuts[cut] // ci, cuts[cut + 1] // ci
        sums = partial_sums(lo, hi)
        for i in range(lo, hi):
            part_out[i * ci : (i + 1) * ci, :] = sums[i - lo].astype(BF16)
        partial_copy(cut).start()

    wait_pieces(half)
    for cut in range(n_cut):
        lo, hi = cuts[cut] // ci, cuts[cut + 1] // ci
        sums = partial_sums(lo, hi)
        for i in range(lo, hi):
            tri[i] = sums[i - lo]
    for cut in range(n_cut):
        partial_copy(cut).wait_recv()
    tri[...] = tri[...] + part_in[...].astype(F32).reshape(ri, ci, CH)
    out_ref[...] = finish_update(1, out_ref[...])

    for q in range(per):
        half_copy(q).wait_send()
    finish_sends(0, slots0)
    for cut in range(n_cut):
        gather_copy(1, slots1, r, cut, 0, beside).wait_send()
        gather_copy(1, slots1, r, cut, 2, other).wait_send()
        gather_copy(1, slots1, theirs, cut, 2, other).wait_send()
        partial_copy(cut).wait_send()
    each_piece(end)


def kernel_body(n_row, pair, chain, in_gain, in_proj, out_gain, out_proj):
    ri, ci, _ = pair.shape
    cells = ri * ci
    piece = -(-ri * ri // 16) * 16
    per = ci // ri
    cuts = (0, (ri // 2 // 2) * 2 * ci, cells)
    n_cut = len(cuts) - 1
    vmem = pl.BlockSpec(memory_space=pltpu.VMEM)
    out = pl.pallas_call(
        functools.partial(kernel, n_row, ri, ci, cuts),
        out_shape=jax.ShapeDtypeStruct((cells, C), BF16),
        in_specs=[pl.BlockSpec(memory_space=pltpu.HBM)] * 6,
        out_specs=vmem,
        scratch_shapes=[
            pltpu.VMEM((cells, C), BF16),
            pltpu.VMEM((1, n_row * ri), jnp.int32),
            pltpu.VMEM(in_gain.shape, F32),
            pltpu.VMEM(in_proj.shape, BF16),
            pltpu.VMEM(out_gain.shape, F32),
            pltpu.VMEM(out_proj.shape, BF16),
            pltpu.SemaphoreType.DMA((6,)),
            pltpu.VMEM((n_row, cells, CH), BF16),
            pltpu.VMEM((n_row, cells, CH), BF16),
            pltpu.VMEM((per, piece, CH), BF16),
            pltpu.VMEM((n_row, piece, CH), BF16),
            pltpu.VMEM((per, piece, CH), F32),
            pltpu.VMEM((ri, ci, CH), F32),
            pltpu.VMEM((n_row, piece, CH), F32),
            pltpu.VMEM((ri, ci, CH), F32),
            pltpu.VMEM((per, piece, CH), BF16),
            pltpu.VMEM((per, piece, CH), BF16),
            pltpu.VMEM((cells, C), F32),
            pltpu.VMEM((cells, 1), F32),
            pltpu.SemaphoreType.DMA((2, 3, n_row, n_cut)),
            pltpu.SemaphoreType.DMA((2, n_row, n_cut)),
            pltpu.SemaphoreType.DMA((per, 2)),
            pltpu.SemaphoreType.DMA((n_row,)),
            pltpu.SemaphoreType.DMA((per,)),
            pltpu.SemaphoreType.DMA((per,)),
            pltpu.VMEM((cells, CH), BF16),
            pltpu.VMEM((cells, CH), BF16),
            pltpu.SemaphoreType.DMA((n_cut,)),
            pltpu.SemaphoreType.DMA((n_cut,)),
        ],
        compiler_params=pltpu.CompilerParams(
            collective_id=0, has_side_effects=True, vmem_limit_bytes=60 * 1024 * 1024
        ),
    )(pair.reshape(cells, C), chain.reshape(1, -1), in_gain, in_proj, out_gain, out_proj)
    return out.reshape(ri, ci, C)


def solution(mesh):
    n_row, n_col = mesh.shape["row"], mesh.shape["col"]
    small = n_col == 2 and n_row == 8
    return jax.shard_map(
        functools.partial(kernel_body, n_row) if small else body,
        mesh=mesh,
        in_specs=(P(("groups", "row"), "col", None), P("groups"), P(), P(), P(), P()),
        out_specs=P(("groups", "row"), "col", None),
        check_vma=False,
    )
```

```python
import functools

import jax
import jax.numpy as jnp
from jax import lax
from jax.experimental import pallas as pl
from jax.experimental.pallas import tpu as pltpu
from jax.sharding import PartitionSpec as P

C = 128
CH = 128
F32 = jnp.float32
BF16 = jnp.bfloat16
MESH = pl.DeviceIdType.MESH


def normalize(values, gain):
    mean = jnp.mean(values, axis=-1, keepdims=True)
    centered = values - mean
    spread = jnp.mean(centered * centered, axis=-1, keepdims=True)
    return centered * lax.rsqrt(spread + 1e-05) * gain


def branch_terms(tile, rows_valid, cols_valid, gain, weights):
    normed = normalize(tile.astype(jnp.float32), gain).astype(jnp.bfloat16)
    flat = normed.reshape(-1, normed.shape[-1])
    proj = jnp.dot(flat, weights, preferred_element_type=jnp.float32)
    proj = proj.reshape(tile.shape[0], tile.shape[1], -1)
    mask = (rows_valid[:, None] * cols_valid[None, :])[:, :, None]
    left = (jax.nn.sigmoid(proj[..., 0:CH]) * proj[..., CH : 2 * CH] * mask).astype(jnp.bfloat16)
    right = (jax.nn.sigmoid(proj[..., 2 * CH : 3 * CH]) * proj[..., 3 * CH : 4 * CH] * mask).astype(
        jnp.bfloat16
    )
    gate = jax.nn.sigmoid(proj[..., 4 * CH : 4 * CH + C])
    return (left, right, gate)


def finish(tile, tri, gate, tri_gain, out_weights):
    tri_normed = normalize(tri, tri_gain).astype(jnp.bfloat16)
    projected = jnp.dot(
        tri_normed.reshape(-1, tri.shape[-1]), out_weights, preferred_element_type=jnp.float32
    )
    update = gate * projected.reshape(gate.shape)
    return (tile.astype(jnp.float32) + update).astype(jnp.bfloat16)


def outgoing(tile, rows_valid, cols_valid, gain, weights, tri_gain, out_weights):
    left, right, gate = branch_terms(tile, rows_valid, cols_valid, gain, weights)
    right_cols = lax.all_gather(right, "row", axis=0, tiled=True)
    right_rows = lax.all_to_all(right_cols, "col", split_axis=0, concat_axis=1, tiled=True)
    tri = jnp.einsum(
        "ikc,jkc->ijc",
        lax.all_gather(left, "col", axis=1, tiled=True),
        right_rows,
        preferred_element_type=jnp.float32,
    )
    return finish(tile, tri, gate, tri_gain, out_weights)


def incoming(tile, rows_valid, cols_valid, gain, weights, tri_gain, out_weights):
    left, right, gate = branch_terms(tile, rows_valid, cols_valid, gain, weights)
    strip = lax.all_gather(left, "col", axis=1, tiled=True)
    left_cols = lax.all_to_all(strip, "row", split_axis=1, concat_axis=0, tiled=True)
    tri = jnp.einsum(
        "kic,kjc->ijc",
        left_cols,
        lax.all_gather(right, "row", axis=0, tiled=True),
        preferred_element_type=jnp.float32,
    )
    return finish(tile, tri, gate, tri_gain, out_weights)


def body(pair, chain, in_gain, in_proj, out_gain, out_proj):
    row_count = pair.shape[0]
    col_count = pair.shape[1]
    valid = (chain >= 0).astype(jnp.float32)
    rows_valid = lax.dynamic_slice_in_dim(valid, lax.axis_index("row") * row_count, row_count, 0)
    cols_valid = lax.dynamic_slice_in_dim(valid, lax.axis_index("col") * col_count, col_count, 0)
    pair_mid = outgoing(
        pair, rows_valid, cols_valid, in_gain[0], in_proj[0], out_gain[0], out_proj[0]
    )
    return incoming(
        pair_mid, rows_valid, cols_valid, in_gain[1], in_proj[1], out_gain[1], out_proj[1]
    )


def layer_norm(values, gain):
    mean = jnp.mean(values, axis=-1, keepdims=True)
    centered = values - mean
    spread = jnp.mean(centered * centered, axis=-1, keepdims=True)
    return (centered * lax.rsqrt(spread + 1e-05) * gain).astype(BF16)


def kernel(
    n_row,
    ri,
    ci,
    cuts,
    pair_hbm,
    chain_hbm,
    in_gain_hbm,
    in_proj_hbm,
    out_gain_hbm,
    out_proj_hbm,
    out_ref,
    pair_ref,
    chain_ref,
    in_gain,
    in_proj,
    out_gain,
    out_proj,
    load_sem,
    slots0,
    slots1,
    piece_out,
    piece_in,
    piece_f32,
    left_f32,
    acc,
    tri,
    half_out,
    half_in,
    gate_ref,
    mask_ref,
    send_sem,
    recv_sem,
    piece_send,
    piece_recv,
    half_send,
    half_recv,
    part_out,
    part_in,
    part_send,
    part_recv,
):
    g = lax.axis_index("groups")
    r = lax.axis_index("row")
    c = lax.axis_index("col")
    n_z = n_row // 2
    per = ci // ri
    z = r // 2
    k = r % 2
    cells = ri * ci

    half = r // per
    inner = (z > 0) & (z < n_z - 1)
    counterpart = (g, (1 - half) * per + r % per, c)
    barrier = pltpu.get_barrier_semaphore()

    def greet(target):
        pl.semaphore_signal(barrier, inc=1, device_id=target, device_id_type=MESH)

    greet((g, r + 1 - 2 * k, c))
    greet((g, r, 1 - c))

    @pl.when(z < n_z - 1)
    def _():
        greet((g, lax.rem(r + 2, n_row), c))

    @pl.when(z > 0)
    def _():
        greet((g, lax.rem(r + n_row - 2, n_row), c))

    sources = (
        (pair_hbm, pair_ref),
        (in_gain_hbm, in_gain),
        (in_proj_hbm, in_proj),
        (chain_hbm, chain_ref),
        (out_gain_hbm, out_gain),
        (out_proj_hbm, out_proj),
    )
    loads = [
        pltpu.make_async_copy(src, dst, load_sem.at[at]) for at, (src, dst) in enumerate(sources)
    ]
    for load in loads:
        load.start()
    for load in loads:
        load.wait()

    shape = (ri, ci, n_row * ri)
    lane = lax.broadcasted_iota(jnp.int32, shape, 2)
    row_at = lax.broadcasted_iota(jnp.int32, shape, 0) + r * ri
    col_at = lax.broadcasted_iota(jnp.int32, shape, 1) + c * ci
    padding = jnp.where(chain_ref[...] < 0, 1.0, 0.0).astype(F32).reshape(1, 1, -1)
    hit = jnp.where((lane == row_at) | (lane == col_at), padding, 0.0)
    mask_ref[...] = 1.0 - jnp.max(hit.reshape(cells, -1), axis=-1, keepdims=True)

    def project(normed, u, first, count):
        return jnp.dot(
            normed,
            in_proj[u, :, first * CH : (first + count) * CH],
            preferred_element_type=F32,
        )

    def gated(both):
        return jax.nn.sigmoid(both[:, :CH]) * both[:, CH:] * mask_ref[...]

    def gather_copy(u, slots, row, cut, way, target):
        lo, hi = cuts[cut], cuts[cut + 1]
        part = slots.at[row, pl.ds(lo, hi - lo)]
        return pltpu.make_async_remote_copy(
            src_ref=part,
            dst_ref=part,
            send_sem=send_sem.at[u, way, row, cut],
            recv_sem=recv_sem.at[u, row, cut],
            device_id=target,
            device_id_type=MESH,
        )

    n_cut = len(cuts) - 1
    up = (g, lax.rem(r + 2, n_row), c)
    down = (g, lax.rem(r + n_row - 2, n_row), c)
    other = (g, r + 1 - 2 * k, c)

    beside = (g, r + 2 - 4 * (z % 2), c)

    def forward(u, slots, row, cut, goes_up, goes_down, act):
        @pl.when(goes_up)
        def _():
            act(gather_copy(u, slots, row, cut, 0, up))

        @pl.when(goes_down)
        def _():
            act(gather_copy(u, slots, row, cut, 1, down))

        act(gather_copy(u, slots, row, cut, 2, other))

    def each_arrival(visit):
        for dist in range(1, n_z):

            @pl.when(z >= dist)
            def _():
                visit(z - dist, 0)

            @pl.when(z + dist < n_z)
            def _():
                visit(z + dist, 1)

    def start(copy):
        copy.start()

    def end(copy):
        copy.wait_send()

    def send_own(u, slots):
        for cut in range(n_cut):
            forward(u, slots, r, cut, z < n_z - 1, z > 0, start)

    def gather(u, slots, work, lag):
        def pass_on(dist):
            for cut in range(n_cut):

                @pl.when(z >= dist)
                def _():
                    mine = 2 * (z - dist) + k
                    gather_copy(u, slots, mine, cut, 0, other).wait_recv()
                    forward(u, slots, mine, cut, z < n_z - 1, False, start)

                @pl.when(z + dist < n_z)
                def _():
                    mine = 2 * (z + dist) + k
                    gather_copy(u, slots, mine, cut, 0, other).wait_recv()
                    forward(u, slots, mine, cut, False, z > 0, start)

        def work_at(z_from):
            work(2 * z_from + k)
            theirs = 2 * z_from + 1 - k
            for cut in range(n_cut):
                gather_copy(u, slots, theirs, cut, 2, other).wait_recv()
            work(theirs)

        def work_dist(dist):
            if dist == 0:
                work_at(z)
                return

            @pl.when(z >= dist)
            def _():
                work_at(z - dist)

            @pl.when(z + dist < n_z)
            def _():
                work_at(z + dist)

        for dist in range(n_z):
            if dist:
                pass_on(dist)
            if dist >= lag:
                work_dist(dist - lag)
        for dist in range(n_z - lag, n_z):
            work_dist(dist)

    def finish_sends(u, slots):
        for cut in range(n_cut):
            forward(u, slots, r, cut, z < n_z - 1, z > 0, end)

        def visit(z_from, side):
            for cut in range(n_cut):
                if side == 0:
                    forward(u, slots, 2 * z_from + k, cut, z < n_z - 1, False, end)
                else:
                    forward(u, slots, 2 * z_from + k, cut, False, z > 0, end)

        each_arrival(visit)

    def finish_update(u, tile):
        normed = layer_norm(tri[...].reshape(cells, CH), out_gain[u : u + 1, :])
        projected = jnp.dot(normed, out_proj[u], preferred_element_type=F32)
        return (tile.astype(F32) + gate_ref[...] * projected).astype(BF16)

    normed = layer_norm(pair_ref[...].astype(F32), in_gain[0:1, :])
    slots0[r] = gated(project(normed, 0, 2, 2)).astype(BF16)

    @pl.when(inner)
    def _():
        pl.semaphore_wait(barrier, 4)

    @pl.when(jnp.logical_not(inner))
    def _():
        pl.semaphore_wait(barrier, 3)

    send_own(0, slots0)
    left_f32[...] = gated(project(normed, 0, 0, 2)).astype(BF16).astype(F32).reshape(ri, ci, CH)
    gate_ref[...] = jax.nn.sigmoid(project(normed, 0, 4, 1))

    def half_copy(q):
        return pltpu.make_async_remote_copy(
            src_ref=half_out.at[q],
            dst_ref=half_in.at[q],
            send_sem=half_send.at[q],
            recv_sem=half_recv.at[q],
            device_id=(g, r, 1 - c),
            device_id_type=MESH,
        )

    def outgoing_block(row):
        block = slots0[row].astype(F32).reshape(ri, ci, CH)
        for i in range(ri):
            acc[row, i * ri : (i + 1) * ri, :] = jnp.sum(left_f32[i][None] * block, axis=1)

        @pl.when(row // per != c)
        def _():
            q = row % per
            half_out[q] = acc[row].astype(BF16)
            half_copy(q).start()

    gather(0, slots0, outgoing_block, 0)
    for q in range(per):
        half_copy(q).wait_recv()
        piece_f32[q] = acc[c * per + q] + half_in[q].astype(F32)
        for i in range(ri):
            tri[i, q * ri : (q + 1) * ri, :] = piece_f32[q, i * ri : (i + 1) * ri, :]
    mid = finish_update(0, pair_ref[...])
    out_ref[...] = mid

    normed = layer_norm(mid.astype(F32), in_gain[1:2, :])
    slots1[r] = gated(project(normed, 1, 2, 2)).astype(BF16)
    for cut in range(n_cut):
        gather_copy(1, slots1, r, cut, 0, beside).start()
        gather_copy(1, slots1, r, cut, 2, other).start()
    left_f32[...] = gated(project(normed, 1, 0, 2)).reshape(ri, ci, CH)
    for q in range(per):
        for kk in range(ri):
            piece_f32[q, kk * ri : (kk + 1) * ri, :] = left_f32[kk, q * ri : (q + 1) * ri, :]
        piece_out[q, :, :] = piece_f32[q].astype(BF16)

    def piece_copy(at, col):
        q = lax.rem(at + 2 * (1 - z % 2), per)
        return pltpu.make_async_remote_copy(
            src_ref=piece_out.at[q],
            dst_ref=piece_in.at[c * per + r % per],
            send_sem=piece_send.at[q, col],
            recv_sem=piece_recv.at[c * per + r % per],
            device_id=(g, half * per + q, col),
            device_id_type=MESH,
        )

    def each_piece(act):
        for at in range(per):
            for col in range(2):
                mine = (lax.rem(at + 2 * (1 - z % 2), per) == r % per) & (c == col)

                @pl.when(jnp.logical_not(mine))
                def _():
                    act(piece_copy(at, col))

    each_piece(start)
    piece_in[c * per + r % per] = piece_out[r % per]
    gate_ref[...] = jax.nn.sigmoid(project(normed, 1, 4, 1))

    theirs = r + 2 - 4 * (z % 2)
    for cut in range(n_cut):
        gather_copy(1, slots1, theirs, cut, 0, beside).wait_recv()
        gather_copy(1, slots1, theirs, cut, 2, other).start()

    def wait_pieces(owner):
        for s in range(per):
            slot = owner * per + s

            @pl.when(slot != c * per + r % per)
            def _():
                pltpu.make_async_remote_copy(
                    src_ref=piece_in.at[slot],
                    dst_ref=piece_in.at[slot],
                    send_sem=piece_send.at[0, 0],
                    recv_sem=piece_recv.at[slot],
                    device_id=other,
                    device_id_type=MESH,
                ).wait_recv()

        for s in range(per):
            piece_f32[s] = piece_in[owner * per + s].astype(F32)

    def partial_sums(lo, hi):
        sums = [jnp.zeros((ci, CH), F32) for _ in range(lo, hi)]
        for s in range(per):
            for kk in range(ri):
                right = slots1[half * per + s, kk * ci : (kk + 1) * ci, :].astype(F32)
                for i in range(lo, hi):
                    at = kk * ri + i
                    sums[i - lo] = sums[i - lo] + right * piece_f32[s, at : at + 1, :]
        return sums

    def partial_copy(cut):
        lo, hi = cuts[cut], cuts[cut + 1]
        return pltpu.make_async_remote_copy(
            src_ref=part_out.at[pl.ds(lo, hi - lo)],
            dst_ref=part_in.at[pl.ds(lo, hi - lo)],
            send_sem=part_send.at[cut],
            recv_sem=part_recv.at[cut],
            device_id=counterpart,
            device_id_type=MESH,
        )

    wait_pieces(1 - half)
    for cut in range(n_cut):
        gather_copy(1, slots1, r + 1 - 2 * k, cut, 2, other).wait_recv()
        gather_copy(1, slots1, theirs + 1 - 2 * k, cut, 2, other).wait_recv()
    for cut in range(n_cut):
        lo, hi = cuts[cut] // ci, cuts[cut + 1] // ci
        sums = partial_sums(lo, hi)
        for i in range(lo, hi):
            part_out[i * ci : (i + 1) * ci, :] = sums[i - lo].astype(BF16)
        partial_copy(cut).start()

    wait_pieces(half)
    for cut in range(n_cut):
        lo, hi = cuts[cut] // ci, cuts[cut + 1] // ci
        sums = partial_sums(lo, hi)
        for i in range(lo, hi):
            tri[i] = sums[i - lo]
    for cut in range(n_cut):
        partial_copy(cut).wait_recv()
    tri[...] = tri[...] + part_in[...].astype(F32).reshape(ri, ci, CH)
    out_ref[...] = finish_update(1, out_ref[...])

    for q in range(per):
        half_copy(q).wait_send()
    finish_sends(0, slots0)
    for cut in range(n_cut):
        gather_copy(1, slots1, r, cut, 0, beside).wait_send()
        gather_copy(1, slots1, r, cut, 2, other).wait_send()
        gather_copy(1, slots1, theirs, cut, 2, other).wait_send()
        partial_copy(cut).wait_send()
    each_piece(end)


def kernel_body(n_row, pair, chain, in_gain, in_proj, out_gain, out_proj):
    ri, ci, _ = pair.shape
    cells = ri * ci
    piece = -(-ri * ri // 16) * 16
    per = ci // ri
    cuts = (0, (ri // 2 // 2) * 2 * ci, cells)
    n_cut = len(cuts) - 1
    vmem = pl.BlockSpec(memory_space=pltpu.VMEM)
    out = pl.pallas_call(
        functools.partial(kernel, n_row, ri, ci, cuts),
        out_shape=jax.ShapeDtypeStruct((cells, C), BF16),
        in_specs=[pl.BlockSpec(memory_space=pltpu.HBM)] * 6,
        out_specs=vmem,
        scratch_shapes=[
            pltpu.VMEM((cells, C), BF16),
            pltpu.VMEM((1, n_row * ri), jnp.int32),
            pltpu.VMEM(in_gain.shape, F32),
            pltpu.VMEM(in_proj.shape, BF16),
            pltpu.VMEM(out_gain.shape, F32),
            pltpu.VMEM(out_proj.shape, BF16),
            pltpu.SemaphoreType.DMA((6,)),
            pltpu.VMEM((n_row, cells, CH), BF16),
            pltpu.VMEM((n_row, cells, CH), BF16),
            pltpu.VMEM((per, piece, CH), BF16),
            pltpu.VMEM((n_row, piece, CH), BF16),
            pltpu.VMEM((per, piece, CH), F32),
            pltpu.VMEM((ri, ci, CH), F32),
            pltpu.VMEM((n_row, piece, CH), F32),
            pltpu.VMEM((ri, ci, CH), F32),
            pltpu.VMEM((per, piece, CH), BF16),
            pltpu.VMEM((per, piece, CH), BF16),
            pltpu.VMEM((cells, C), F32),
            pltpu.VMEM((cells, 1), F32),
            pltpu.SemaphoreType.DMA((2, 3, n_row, n_cut)),
            pltpu.SemaphoreType.DMA((2, n_row, n_cut)),
            pltpu.SemaphoreType.DMA((per, 2)),
            pltpu.SemaphoreType.DMA((n_row,)),
            pltpu.SemaphoreType.DMA((per,)),
            pltpu.SemaphoreType.DMA((per,)),
            pltpu.VMEM((cells, CH), BF16),
            pltpu.VMEM((cells, CH), BF16),
            pltpu.SemaphoreType.DMA((n_cut,)),
            pltpu.SemaphoreType.DMA((n_cut,)),
        ],
        compiler_params=pltpu.CompilerParams(
            collective_id=0, has_side_effects=True, vmem_limit_bytes=60 * 1024 * 1024
        ),
    )(pair.reshape(cells, C), chain.reshape(1, -1), in_gain, in_proj, out_gain, out_proj)
    return out.reshape(ri, ci, C)


def solution(mesh):
    n_row, n_col = mesh.shape["row"], mesh.shape["col"]
    small = n_col == 2 and n_row == 8
    return jax.shard_map(
        functools.partial(kernel_body, n_row) if small else body,
        mesh=mesh,
        in_specs=(P(("groups", "row"), "col", None), P("groups"), P(), P(), P(), P()),
        out_specs=P(("groups", "row"), "col", None),
        check_vma=False,
    )
```
